32 devices in a mesh: expert: 8 (over z, y), shard: 4 (over x, core).
Axes of the slice: x: 2, y: 2, z: 4, core: 2. Of those that a mesh axis runs over, the one named last changes fastest.
Arguments:
- tokens: bfloat16 [16384, 768], P(('expert', 'shard')), may hold values from -6 to 6
- w_qkv: bfloat16 [768, 2304], P('shard'), may hold values from -0.21875 to 0.21875
- w_out: bfloat16 [768, 768], P('shard'), may hold values from -0.875 to 0.875
- router: bfloat16 [768, 8], P('shard'), may hold values from -0.15625 to 0.15625
- gain_attn: bfloat16 [768], P('shard'), may hold values from 0.099609375 to 1.8984375
- gain_ffn: bfloat16 [768], P('shard'), may hold values from 0.099609375 to 1.8984375
- rel_bias: bfloat16 [12, 32], P('shard'), may hold values from -4 to 4
- w_gate: bfloat16 [8, 768, 3072], P('expert', None, 'shard'), may hold values from -0.21875 to 0.21875
- w_up: bfloat16 [8, 768, 3072], P('expert', None, 'shard'), may hold values from -0.21875 to 0.21875
- w_down: bfloat16 [8, 3072, 768], P('expert', 'shard'), may hold values from -0.109375 to 0.109375
- routes: int32 [16384, 2], P(('expert', 'shard')), may hold values from 0 to 7, all different within a row; in each aligned block of 512 rows (0 to 511, 512 to 1023, ...) at most 256 rows name the same one
- lengths: int32 [8, 3], P('expert'), may hold values from 1 to 1792, 2048 in all within a row
- cotangent: bfloat16 [16384, 768], P(('expert', 'shard')), may hold values from -6 to 6
Outputs:
- output: bfloat16 [16384, 768], P(('expert', 'shard'))
- grad_tokens: float32 [16384, 768], P(('expert', 'shard'))
- grad_qkv: float32 [768, 2304], P('shard')
- grad_out: float32 [768, 768], P('shard')
- grad_router: float32 [768, 8], P('shard')
- grad_gain_attn: float32 [768], P('shard')
- grad_gain_ffn: float32 [768], P('shard')
- grad_rel_bias: float32 [12, 32], P('shard')
- grad_gate: float32 [8, 768, 3072], P('expert', None, 'shard')
- grad_up: float32 [8, 768, 3072], P('expert', None, 'shard')
- grad_down: float32 [8, 3072, 768], P('expert', 'shard')
The draws below stay inside these ranges and needn't reach their ends.
Inputs may be any that keep to these rules, and one draw needn't show every extreme that they name: `routes`: each row names 2 different experts; among the 512 rows of one device no expert is named more than 256 times. Row g gives the lengths of the 3 sequences of group g, which holds the 2048 tokens of 4 consecutive devices in order; each row sums to 2048 and its largest entry is 1792.
All inputs are finite; a program needn't handle non-finite values.
Results may differ from the reference program's by a relative error of at most 0.019.
Values may be sent and summed in bfloat16 or wider, within the bound.
A program may use at most 384 MiB of HBM per device.

```python
import math
import jax
import jax.numpy as jnp
import numpy as np
from jax import lax

D = 768
HEADS = 12
HEAD_DIM = 64
FF = 3072
TOP = 2
BUCKETS = 32
SEQS = 3
TOK_DEV = 512
EXPERTS = 8
GROUP_TOK = 2048
LONGEST = 1792
CAP = 256
TOKENS = 16384
N_EXPERT = 8
DEVICES = 32


def shard_levels(key, extent, cuts, low, high):
    level, own = 1.0, jax.random.fold_in(key, 6)
    for dim, shards_of in cuts:
        draws = jnp.exp(jax.random.uniform(jax.random.fold_in(own, dim), (shards_of,), jnp.float32, low / len(cuts), high / len(cuts)))
        level = level * jnp.repeat(draws, extent[dim] // shards_of).reshape([-1 if axis == dim else 1 for axis in range(len(extent))])
    return level


def profile(amount, total, bound, slope):
    weights = [(1 << 20) // math.isqrt(rank ** slope) + 1 for rank in range(2, amount + 1)]
    spare, given = total - bound - (amount - 1), [1] * (amount - 1)
    while spare > 0:
        candidates = [i for i in range(amount - 1) if given[i] < bound]
        mass, remaining = sum([weights[i] for i in candidates]), spare
        for i in candidates:
            more = min(bound - given[i], max(1, remaining * weights[i] // mass), spare)
            given[i] = given[i] + more
            spare = spare - more
    return np.array([bound] + given)


def ragged_sizes(stream_key, amount, total, limit, slope):
    if amount == 2:
        one = jax.random.randint(stream_key, (), max(1, total - limit), min(limit, total - 1) + 1)
        return jnp.stack([one, total - one])
    sizes = jnp.asarray(profile(amount, total, limit, slope), jnp.int32)
    couples = (amount - 1) // 2
    source_of, receiver = sizes[1:1 + 2 * couples:2], sizes[2:2 + 2 * couples:2]
    slack = jnp.minimum(source_of - 1, limit - receiver)
    shifted = jax.random.randint(jax.random.fold_in(stream_key, 1), (couples,), 0, 1 << 20) % (slack + 1)
    sizes = sizes.at[1:1 + 2 * couples:2].set(source_of - shifted).at[2:2 + 2 * couples:2].set(receiver + shifted)
    return sizes[jax.random.permutation(jax.random.fold_in(stream_key, 2), amount)]


def deal_out(key, own, number, rows, count, top, limit, lean):
    order = jax.random.permutation(key, count)
    packed, usual = shares(count, rows * top, limit, lean, True), shares(count, rows * top, limit, lean, False)
    places = jnp.arange(count)

    def named(sizes, rotation):
        used = int((sizes > 0).sum())
        fixed = max(1, used // 4)
        passed = fixed + (places - fixed + rotation * (used - fixed)) % max(1, count - fixed)
        return jnp.zeros((count,), jnp.int32).at[order[jnp.where(places < fixed, places, passed)]].set(jnp.asarray(sizes, jnp.int32))

    sizes = jnp.where(number % 4 == 0, named(packed, number // 4), named(usual, number - number // 4 - 1))
    mixed = jax.random.permutation(jax.random.fold_in(own, 3), count)
    donor, sink = mixed[0:count // 2 * 2:2], mixed[1:count // 2 * 2:2]
    margin = jnp.minimum(sizes[donor] - 1, limit - sizes[sink]) // 2
    margin = jnp.where((donor == order[0]) | (sink == order[0]) | (sizes[sink] == 0), 0, jnp.maximum(margin, 0))
    passed = jax.random.randint(jax.random.fold_in(own, 4), (count // 2,), 0, 1 << 20) % (margin + 1)
    sizes = sizes.at[donor].add(-passed).at[sink].add(passed)
    items = jnp.searchsorted(jnp.cumsum(sizes), jnp.arange(rows * top), side="right").astype(jnp.int32)
    grid = items.reshape(top, rows).T
    grid = grid[jax.random.permutation(jax.random.fold_in(own, 1), rows)]
    rotation = jax.random.randint(jax.random.fold_in(own, 2), (rows, 1), 0, top)
    return jnp.take_along_axis(grid, (jnp.arange(top)[None, :] + rotation) % top, axis=1)


def shares(number_of, total, reach, slope, full):
    loads = [(1 << 20) // math.isqrt(grade ** slope) + 1 for grade in range(1, number_of + 1)]
    largest = reach if full else min(reach, max(-(-total // number_of), total * loads[0] // sum(loads)))
    least = 1 if total - largest >= number_of - 1 else 0
    counts, surplus = [largest] + [least] * (number_of - 1), total - largest - least * (number_of - 1)
    while surplus > 0:
        candidates = [i for i in range(1, number_of) if counts[i] < largest] or [i for i in range(1, number_of) if counts[i] < reach]
        mass, remaining = sum([loads[i] for i in candidates]), surplus
        for i in candidates:
            more = min(reach - counts[i], max(1, remaining * loads[i] // mass), surplus)
            counts[i] = counts[i] + more
            surplus = surplus - more
    return np.array(counts)


def scatter_about(stream_key, extent, deviation, most, cuts=(), held_as=jnp.bfloat16):
    factor_of = shard_levels(stream_key, extent, cuts, -0.22, 0.18) if cuts else 1.0
    values = jax.random.normal(stream_key, extent, jnp.float32) * deviation * factor_of
    return jnp.minimum(jnp.maximum(values, -most), most).astype(held_as)


def setup_inputs(seed: int = 0) -> dict:
    streams_of = jax.random.split(jax.random.key(seed), 14)
    tokens = scatter_about(streams_of[0], (TOKENS, D), 1.0, 6.0, ((0, 32),))
    w_qkv = scatter_about(streams_of[1], (D, 3 * D), D ** -0.5, 0.21875, ((0, 4),))
    w_out = scatter_about(streams_of[2], (D, D), (D // 16) ** -0.5, 0.875, ((0, 4),))
    router = scatter_about(streams_of[3], (D, EXPERTS), (2 * D) ** -0.5, 0.15625, ((0, 4),))
    gain_attn = jnp.clip(1.0 + 0.18 * jax.random.normal(streams_of[4], (D,), jnp.float32), 0.099609375, 1.8984375).astype(jnp.bfloat16)
    gain_ffn = jnp.clip(1.0 + 0.18 * jax.random.normal(streams_of[5], (D,), jnp.float32), 0.099609375, 1.8984375).astype(jnp.bfloat16)
    rel_bias = scatter_about(streams_of[6], (HEADS, BUCKETS), 1.0, 4.0, ((0, 4),))
    w_gate = scatter_about(streams_of[7], (EXPERTS, D, FF), D ** -0.5, 0.21875, ((0, 8), (2, 4)))
    w_up = scatter_about(streams_of[8], (EXPERTS, D, FF), D ** -0.5, 0.21875, ((0, 8), (2, 4)))
    w_down = scatter_about(streams_of[9], (EXPERTS, FF, D), FF ** -0.5, 0.109375, ((0, 8), (1, 4)))
    routes_keys = jax.random.split(jax.random.fold_in(streams_of[10], 1), TOKENS // TOK_DEV)
    routes_turns = jax.random.permutation(jax.random.fold_in(streams_of[10], 3), TOKENS // TOK_DEV)
    routes = jax.vmap(lambda own, number: deal_out(jax.random.fold_in(streams_of[10], 2), own, number, TOK_DEV, EXPERTS, TOP, CAP, 1))(routes_keys, routes_turns).reshape((TOKENS, TOP))
    lengths = jax.vmap(lambda own: ragged_sizes(own, SEQS, GROUP_TOK, LONGEST, 2))(jax.random.split(streams_of[11], N_EXPERT)).reshape((N_EXPERT, SEQS)).astype(jnp.int32)
    cotangent = scatter_about(streams_of[12], (TOKENS, D), 1.0, 6.0, ((0, 32),))
    return dict(tokens=tokens, w_qkv=w_qkv, w_out=w_out, router=router, gain_attn=gain_attn, gain_ffn=gain_ffn, rel_bias=rel_bias, w_gate=w_gate, w_up=w_up, w_down=w_down, routes=routes, lengths=lengths, cotangent=cotangent)


norm_epsilon = 1e-06
highest = lax.Precision.HIGHEST
bucket_borders = (16, 23, 32, 45, 64, 91, 128, 181, 256, 362, 512, 724, 1024, 1448, 2048, 2896)

@jax.custom_vjp
def low(v):
    return lax.optimization_barrier(v.astype(jnp.bfloat16)).astype(jnp.float32)

@jax.custom_vjp
def low_back(v):
    return v

def low_keep(v):
    return (low(v), None)

def low_pass(kept, grad):
    return (grad,)

def back_keep(v):
    return (v, None)

def back_low(kept, grad):
    return (low(grad),)
low.defvjp(low_keep, low_pass)
low_back.defvjp(back_keep, back_low)

def bucket_of(distance):
    clipped = jnp.maximum(distance, 0)
    bucket_id = jnp.minimum(clipped, 15)
    for border in bucket_borders:
        bucket_id = bucket_id + (clipped >= border).astype(jnp.int32)
    return bucket_id

def rms_norm(values, gain_vector):
    inverse = lax.rsqrt(lax.optimization_barrier(jnp.mean(values * values, axis=-1, keepdims=True)) + norm_epsilon)
    return values * inverse * gain_vector

def gated_unit(gate_value, up_value):
    return jax.nn.gelu(gate_value) * up_value

def route_slots(routes):
    flat_routes = routes.reshape(DEVICES, TOK_DEV * TOP)
    expert_ids = jnp.arange(EXPERTS, dtype=jnp.int32)
    onehot_rows = (flat_routes[:, :, None] == expert_ids[None, None, :]).astype(jnp.int32)
    earlier = jnp.cumsum(onehot_rows, axis=1) - onehot_rows
    position = lax.optimization_barrier(jnp.sum(earlier * onehot_rows, axis=2))
    device_ids = jnp.arange(DEVICES, dtype=jnp.int32)[:, None]
    return (device_ids * CAP + position).reshape(-1).astype(jnp.int32)

def group_attention(group_qkv, group_lengths, bias_table):
    query_heads = group_qkv[:, 0]
    key_heads = group_qkv[:, 1]
    value_heads = group_qkv[:, 2]
    positions = jnp.arange(GROUP_TOK, dtype=jnp.int32)
    seq_ends = jnp.cumsum(group_lengths).astype(jnp.int32)
    sequence = lax.optimization_barrier(jnp.sum((positions[:, None] >= seq_ends[None, :]).astype(jnp.int32), axis=1))
    distance = positions[:, None] - positions[None, :]
    allowed = (sequence[:, None] == sequence[None, :]) & (distance >= 0)
    products = low_back(jnp.einsum('qhd,khd->hqk', query_heads, key_heads, precision=highest))
    scores = products * HEAD_DIM ** (-0.5) + bias_table[:, bucket_of(distance)]
    softmax_weights = jax.nn.softmax(jnp.where(allowed[None], scores, -1e+30), axis=-1)
    blended = jnp.einsum('hqk,khd->qhd', low(softmax_weights), value_heads, precision=highest)
    return low_back(low(blended)).reshape(GROUP_TOK, HEADS * HEAD_DIM)

def expert_unit(operands):
    rows_in, gate_weight, up_weight, down_weight = operands
    gate_proj = low_back(jnp.dot(rows_in, gate_weight, precision=highest))
    up_proj = low_back(jnp.dot(rows_in, up_weight, precision=highest))
    hidden = low(gated_unit(gate_proj, up_proj))
    return low_back(low(jnp.dot(hidden, down_weight, precision=highest)))

def reference(tokens, w_qkv, w_out, router, gain_attn, gain_ffn, rel_bias, w_gate, w_up, w_down, routes, lengths, cotangent):
    slot_rows = route_slots(routes)
    flat_experts = routes.reshape(-1).astype(jnp.int32)

    def forward(inputs, qkv_weight, out_weight, router_weight, attn_gain, ffn_gain, bias_table, gate_weight, up_weight, down_weight):
        normed = low(rms_norm(inputs, attn_gain))
        qkv = low_back(low(jnp.dot(normed, qkv_weight, precision=highest)))
        grouped = qkv.reshape(N_EXPERT, GROUP_TOK, 3, HEADS, HEAD_DIM)

        def one_group(operands):
            group_qkv, group_lengths = operands
            return group_attention(group_qkv, group_lengths, bias_table)
        attended = lax.map(jax.checkpoint(one_group), (grouped, lengths)).reshape(TOKENS, D)
        hidden_one = inputs + low_back(jnp.dot(attended, out_weight, precision=highest))
        normed_ffn = low(rms_norm(hidden_one, ffn_gain))
        logits = low_back(jnp.dot(normed_ffn, router_weight, precision=highest))
        gate_weights = jax.nn.softmax(jnp.take_along_axis(logits, routes, axis=1), axis=1)
        copies = low_back(jnp.repeat(normed_ffn, TOP, axis=0))
        buffer = jnp.zeros((EXPERTS, DEVICES * CAP, D), jnp.float32).at[flat_experts, slot_rows].set(copies)
        results = lax.map(jax.checkpoint(expert_unit), (buffer, gate_weight, up_weight, down_weight))
        picked = results[flat_experts, slot_rows].reshape(TOKENS, TOP, D)
        return hidden_one + lax.optimization_barrier(jnp.sum(gate_weights[:, :, None] * picked, axis=1))
    operands = (tokens, w_qkv, w_out, router, gain_attn, gain_ffn, rel_bias, w_gate, w_up, w_down)
    floats = tuple((item.astype(jnp.float32) for item in operands))
    mixed_out, pullback = jax.vjp(forward, *floats)
    gradients = pullback(cotangent.astype(jnp.float32))
    return (mixed_out.astype(jnp.bfloat16), gradients[0], gradients[1], gradients[2], gradients[3], gradients[4], gradients[5], gradients[6], gradients[7], gradients[8], gradients[9])
```

```python
import functools

import jax
import jax.numpy as jnp
from jax import lax
from jax.experimental import pallas as pl
from jax.experimental.pallas import tpu as pltpu
from jax.sharding import PartitionSpec as P

norm_epsilon = 1e-06
bucket_borders = (16, 23, 32, 45, 64, 91, 128, 181, 256, 362, 512, 724, 1024, 1448, 2048, 2896)


def bucket_of(distance):
    clipped = jnp.maximum(distance, 0)
    bucket_id = jnp.minimum(clipped, 15)
    for border in bucket_borders:
        bucket_id = bucket_id + (clipped >= border).astype(jnp.int32)
    return bucket_id


tile = 256
low_score = -1e30


def toeplitz_vectors(bias_table, diagonals):
    offsets = jnp.arange(2 * tile, dtype=jnp.int32)
    offsets = jnp.where(offsets < tile, offsets, offsets - 2 * tile)
    distance = jnp.arange(diagonals, dtype=jnp.int32)[:, None] * tile + offsets[None, :]
    onehot = bucket_of(distance)[None] == jnp.arange(bias_table.shape[1])[:, None, None]
    return jnp.einsum(
        "hc,cdm->hdm", bias_table, onehot.astype(jnp.bfloat16), preferred_element_type=jnp.float32
    )


def fill_bias(vector_ref, head, bias_ref, diagonals):
    def fill(delta, carry):
        row = vector_ref[head, pl.ds(delta, 1), :]
        wide = jnp.broadcast_to(row, (tile, 2 * tile))
        rolled = pltpu.roll(wide, 0, 1, stride=1, stride_axis=0)
        bias_ref[delta] = rolled[:, :tile]
        return carry

    lax.fori_loop(0, diagonals, fill, 0)


def start_of(position, first_end, second_end):
    return jnp.where(
        position >= second_end, second_end, jnp.where(position >= first_end, first_end, 0)
    )


def contract(left, right, left_dim, right_dim):
    return lax.dot_general(
        left, right, (((left_dim,), (right_dim,)), ((), ())), preferred_element_type=jnp.float32
    )


def attend_kernel(info_ref, q_ref, k_ref, v_ref, vector_ref, out_ref, log_ref, bias_ref, side_ref):
    diagonals = vector_ref.shape[1]
    query_tiles = q_ref.shape[0] // tile
    lanes = lax.broadcasted_iota(jnp.int32, (1, 128), 1)
    for head in range(2):
        mine = (lanes < 64) if head == 0 else (lanes >= 64)
        fill_bias(vector_ref, head, bias_ref, diagonals)
        for block in range(query_tiles):
            rows = pl.ds(block * tile, tile)
            query_tile = info_ref[2] * query_tiles + block
            query = jnp.where(mine, q_ref[rows, :] * 0.125, 0).astype(jnp.bfloat16)
            first_end, second_end = info_ref[0], info_ref[1]
            first_tile = start_of(query_tile * tile, first_end, second_end) // tile
            query_pos = query_tile * tile + lax.broadcasted_iota(jnp.int32, (1, tile), 1)
            query_start = start_of(query_pos, first_end, second_end)

            def step(index, carry):
                top, total = carry
                keys = pl.ds(pl.multiple_of(index * tile, tile), tile)
                key_pos = index * tile + lax.broadcasted_iota(jnp.int32, (tile, 1), 0)
                scores = contract(k_ref[keys, :], query, 1, 1) + bias_ref[query_tile - index]
                allowed = (key_pos >= query_start) & (key_pos <= query_pos)
                scores = jnp.where(allowed, scores, low_score)
                new_top = jnp.maximum(top, jnp.max(scores, axis=0, keepdims=True))
                weights = jnp.exp(scores - new_top).astype(jnp.bfloat16)
                value = jnp.where(mine, v_ref[keys, :], 1).astype(jnp.bfloat16)
                part = contract(value, weights, 0, 0)
                return new_top, total * jnp.exp(top - new_top) + part

            top, total = lax.fori_loop(
                first_tile,
                query_tile + 1,
                step,
                (jnp.full((1, tile), low_score, jnp.float32), jnp.zeros((128, tile), jnp.float32)),
            )
            if head == 0:
                row_total = total[64:65]
                side_ref[0:64, rows] = total[0:64] / row_total
            else:
                row_total = total[0:1]
                side_ref[64:128, rows] = total[64:128] / row_total
            log_ref[0, head : head + 1, rows] = top + jnp.log(row_total)
    for block in range(query_tiles):
        rows = pl.ds(block * tile, tile)
        out_ref[rows, :] = side_ref[:, rows].T.astype(jnp.bfloat16)


def attend_back_kernel(
    info_ref,
    q_ref,
    k_ref,
    v_ref,
    g_ref,
    o_ref,
    log_ref,
    vector_ref,
    dq_ref,
    dk_ref,
    dv_ref,
    diag_ref,
    bias_ref,
    grad_bias_ref,
    dk_acc,
    dv_acc,
    dq_acc,
):
    diagonals = vector_ref.shape[1]
    query_tiles = q_ref.shape[0] // tile
    lanes = lax.broadcasted_iota(jnp.int32, (1, 128), 1)
    dk_acc[...] = jnp.zeros_like(dk_acc)
    dv_acc[...] = jnp.zeros_like(dv_acc)
    dq_acc[...] = jnp.zeros_like(dq_acc)
    for head in range(2):
        mine = (lanes < 64) if head == 0 else (lanes >= 64)
        fill_bias(vector_ref, head, bias_ref, diagonals)
        grad_bias_ref[...] = jnp.zeros_like(grad_bias_ref)
        for block in range(query_tiles):
            rows = pl.ds(block * tile, tile)
            query_tile = info_ref[2] * query_tiles + block
            query = jnp.where(mine, q_ref[rows, :] * 0.125, 0).astype(jnp.bfloat16)
            grad = jnp.where(mine, g_ref[rows, :], 0).astype(jnp.bfloat16)
            product = grad.astype(jnp.float32) * o_ref[rows, :].astype(jnp.float32)
            delta_row = jnp.sum(product.T, axis=0, keepdims=True)
            log_row = log_ref[0, head : head + 1, rows]
            first_end, second_end = info_ref[0], info_ref[1]
            first_tile = start_of(query_tile * tile, first_end, second_end) // tile
            query_pos = query_tile * tile + lax.broadcasted_iota(jnp.int32, (1, tile), 1)
            query_start = start_of(query_pos, first_end, second_end)

            def step(index, carry):
                keys = pl.ds(pl.multiple_of(index * tile, tile), tile)
                key_pos = index * tile + lax.broadcasted_iota(jnp.int32, (tile, 1), 0)
                key = k_ref[keys, :]
                scores = contract(key, query, 1, 1) + bias_ref[query_tile - index]
                allowed = (key_pos >= query_start) & (key_pos <= query_pos)
                probs = jnp.exp(jnp.where(allowed, scores - log_row, low_score))
                grad_probs = contract(v_ref[keys, :], grad, 1, 1)
                grad_scores = probs * (grad_probs - delta_row)
                grad_bias_ref[query_tile - index] += grad_scores
                low = grad_scores.astype(jnp.bfloat16)
                dv_acc[keys, :] += contract(probs.astype(jnp.bfloat16), grad, 1, 0)
                dk_acc[keys, :] += contract(low, query, 1, 0)
                key_mine = jnp.where(mine, key, 0).astype(jnp.bfloat16)
                dq_acc[rows, :] += contract(low, key_mine, 0, 0)
                return carry

            lax.fori_loop(first_tile, query_tile + 1, step, 0)

        def reduce(delta, carry):
            value = grad_bias_ref[delta]
            value = jnp.concatenate([value, jnp.zeros_like(value)], axis=1)
            half = tile // 2
            while half >= 8:
                value = value[:half] + pltpu.roll(value[half:], 2 * tile - half, 1)
                half //= 2
            diag_ref[head, delta] = value
            return carry

        lax.fori_loop(0, diagonals, reduce, 0)
    dq_ref[...] = (dq_acc[...] * 0.125).astype(jnp.bfloat16)
    dk_ref[...] = dk_acc[...].astype(jnp.bfloat16)
    dv_ref[...] = dv_acc[...].astype(jnp.bfloat16)


def head_specs(tok_count, group_tok, model_width):
    pairs = model_width // 128
    return (
        pl.BlockSpec(memory_space=pltpu.SMEM),
        pl.BlockSpec((tok_count, 128), lambda p: (0, p)),
        pl.BlockSpec((group_tok, 128), lambda p: (0, p)),
        pl.BlockSpec((group_tok, 128), lambda p: (0, p + pairs)),
    )


def attend(info, qkv, kv, vectors):
    tok_count, group_tok, model_width = qkv.shape[0], kv.shape[0], kv.shape[1] // 2
    pairs, diagonals = model_width // 128, vectors.shape[1]
    cost = 4 * tok_count * group_tok * model_width
    return pl.pallas_call(
        attend_kernel,
        grid=(pairs,),
        in_specs=[
            *head_specs(tok_count, group_tok, model_width),
            pl.BlockSpec((2, diagonals, 2 * tile), lambda p: (p, 0, 0)),
        ],
        out_specs=[
            pl.BlockSpec((tok_count, 128), lambda p: (0, p)),
            pl.BlockSpec((1, 2, tok_count), lambda p: (p, 0, 0)),
        ],
        out_shape=[
            jax.ShapeDtypeStruct((tok_count, model_width), jnp.bfloat16),
            jax.ShapeDtypeStruct((pairs, 2, tok_count), jnp.float32),
        ],
        scratch_shapes=[
            pltpu.VMEM((diagonals, tile, tile), jnp.float32),
            pltpu.VMEM((128, tok_count), jnp.float32),
        ],
        compiler_params=pltpu.CompilerParams(vmem_limit_bytes=40 * 2**20),
        cost_estimate=pl.CostEstimate(
            flops=16 * cost, bytes_accessed=4 * group_tok * model_width, transcendentals=0
        ),
        name="attend",
    )(info, qkv, kv, kv, vectors)


def attend_back(info, qkv, kv, grad, attended, logs, vectors):
    tok_count, group_tok, model_width = qkv.shape[0], kv.shape[0], kv.shape[1] // 2
    pairs, diagonals = model_width // 128, vectors.shape[1]
    cost = 10 * tok_count * group_tok * model_width
    query_spec = pl.BlockSpec((tok_count, 128), lambda p: (0, p))
    key_spec = pl.BlockSpec((group_tok, 128), lambda p: (0, p))
    return pl.pallas_call(
        attend_back_kernel,
        grid=(pairs,),
        in_specs=[
            *head_specs(tok_count, group_tok, model_width),
            query_spec,
            query_spec,
            pl.BlockSpec((1, 2, tok_count), lambda p: (p, 0, 0)),
            pl.BlockSpec((2, diagonals, 2 * tile), lambda p: (p, 0, 0)),
        ],
        out_specs=[
            query_spec,
            key_spec,
            key_spec,
            pl.BlockSpec((2, diagonals, 8, 2 * tile), lambda p: (p, 0, 0, 0)),
        ],
        out_shape=[
            jax.ShapeDtypeStruct((tok_count, model_width), jnp.bfloat16),
            jax.ShapeDtypeStruct((group_tok, model_width), jnp.bfloat16),
            jax.ShapeDtypeStruct((group_tok, model_width), jnp.bfloat16),
            jax.ShapeDtypeStruct((2 * pairs, diagonals, 8, 2 * tile), jnp.float32),
        ],
        scratch_shapes=[
            pltpu.VMEM((diagonals, tile, tile), jnp.float32),
            pltpu.VMEM((diagonals, tile, tile), jnp.float32),
            pltpu.VMEM((group_tok, 128), jnp.float32),
            pltpu.VMEM((group_tok, 128), jnp.float32),
            pltpu.VMEM((tok_count, 128), jnp.float32),
        ],
        compiler_params=pltpu.CompilerParams(vmem_limit_bytes=48 * 2**20),
        cost_estimate=pl.CostEstimate(
            flops=10 * cost, bytes_accessed=8 * group_tok * model_width, transcendentals=0
        ),
        name="attend_back",
    )(info, qkv, kv, kv, grad, attended, logs, vectors)


def table_gradient(diag, bucket_count):
    head_count, diagonals, fold, width = diag.shape
    offsets = jnp.arange(width, dtype=jnp.int32)
    offsets = jnp.where(offsets < tile, offsets, offsets - width)
    distance = (
        jnp.arange(diagonals, dtype=jnp.int32)[:, None, None] * tile
        + offsets[None, None, :]
        - jnp.arange(fold, dtype=jnp.int32)[None, :, None]
    )
    onehot = bucket_of(distance)[None] == jnp.arange(bucket_count)[:, None, None, None]
    return jnp.einsum(
        "hdrc,bdrc->hb",
        diag,
        onehot.astype(jnp.float32),
        precision=lax.Precision.HIGHEST,
        preferred_element_type=jnp.float32,
    )


def partner(value, flip):
    count = lax.axis_size("shard")
    return lax.ppermute(value, "shard", [(i, i ^ flip) for i in range(count)])


def gather_pieces(value):
    across = partner(value, 2)
    return [value, partner(value, 1), across, partner(across, 1)]


def reduce_pieces(pieces):
    low = [p.astype(jnp.bfloat16) for p in pieces]
    far = (pieces[2] + partner(low[3], 1).astype(jnp.float32)).astype(jnp.bfloat16)
    near = pieces[0] + partner(low[1], 1).astype(jnp.float32)
    return near + partner(far, 2).astype(jnp.float32)


def reduce_rows(value, shard_index):
    count = lax.axis_size("shard")
    split = value.reshape(count, value.shape[0] // count, *value.shape[1:])
    return reduce_pieces(
        [
            lax.dynamic_index_in_dim(split, shard_index ^ r, 0, keepdims=False).astype(jnp.float32)
            for r in range(count)
        ]
    )


def dot32(left, right, spec):
    return jnp.einsum(spec, left, right, preferred_element_type=jnp.float32)


def norm_forward(values):
    inverse = lax.rsqrt(jnp.mean(values * values, axis=-1, keepdims=True) + norm_epsilon)
    return (values * inverse, inverse)


def norm_backward(grad_normed, normalized, inverse, gain_vector):
    grad_gain = jnp.sum(grad_normed * normalized, axis=0)
    scaled = grad_normed * gain_vector
    grad_values = inverse * (
        scaled - normalized * jnp.mean(scaled * normalized, axis=-1, keepdims=True)
    )
    return (grad_values, grad_gain)


def gated_unit(gate_value, up_value):
    return jax.nn.gelu(gate_value) * up_value


def local(
    tokens,
    w_qkv,
    w_out,
    router,
    gain_attn,
    gain_ffn,
    rel_bias,
    w_gate,
    w_up,
    w_down,
    routes,
    lengths,
    cotangent,
):
    shard_index = lax.axis_index("shard")
    full_qkv, full_out, full_router, full_gain_attn, full_gain_ffn, full_table = (
        lax.all_gather(w_qkv, "shard", axis=0, tiled=True),
        lax.all_gather(w_out, "shard", axis=0, tiled=True),
        lax.all_gather(router, "shard", axis=0, tiled=True),
        lax.all_gather(gain_attn, "shard", axis=0, tiled=True),
        lax.all_gather(gain_ffn, "shard", axis=0, tiled=True),
        lax.all_gather(rel_bias, "shard", axis=0, tiled=True),
    )
    tok_count, model_width = tokens.shape
    head_count, bucket_count = full_table.shape
    expert_count = full_router.shape[1]
    route_count = routes.shape[1]
    capacity = 2 * route_count * tok_count // expert_count
    inputs = tokens.astype(jnp.float32)
    attn_gain = full_gain_attn.astype(jnp.float32)
    ffn_gain = full_gain_ffn.astype(jnp.float32)
    normed_one, inverse_one = norm_forward(inputs)
    normed_attn = (normed_one * attn_gain).astype(jnp.bfloat16)
    qkv = jnp.dot(normed_attn, full_qkv, preferred_element_type=jnp.float32).astype(jnp.bfloat16)
    kv = lax.all_gather(qkv[:, model_width:], "shard", axis=0, tiled=True)
    group_tok = kv.shape[0]
    info = jnp.stack([lengths[0, 0], lengths[0, 0] + lengths[0, 1], shard_index]).astype(jnp.int32)
    vectors = toeplitz_vectors(full_table, group_tok // tile)
    weights_in, kv = lax.optimization_barrier(((w_gate[0], w_up[0], w_down[0]), kv))
    gate_pieces, up_pieces, down_pieces = (gather_pieces(w) for w in weights_in)
    attended, logs = attend(info, qkv, kv, vectors)
    hidden_one = inputs + jnp.dot(attended, full_out, preferred_element_type=jnp.float32)
    normed_two, inverse_two = norm_forward(hidden_one)
    normed_ffn = (normed_two * ffn_gain).astype(jnp.bfloat16)
    logits = jnp.dot(normed_ffn, full_router, preferred_element_type=jnp.float32)
    expert_ids = jnp.arange(expert_count, dtype=jnp.int32)
    chosen_mask = routes[:, :, None] == expert_ids[None, None, :]
    chosen = jnp.sum(jnp.where(chosen_mask, logits[:, None, :], 0.0), axis=2)
    gate_weights = jax.nn.softmax(chosen, axis=1)
    flat_routes = routes.reshape(-1)
    onehot_rows = (flat_routes[:, None] == expert_ids[None, :]).astype(jnp.int32)
    earlier = jnp.cumsum(onehot_rows, axis=0) - onehot_rows
    position = jnp.sum(earlier * onehot_rows, axis=1)
    slot_index = flat_routes * capacity + position
    slot_pair = slot_index.reshape(tok_count, route_count)
    slots = jnp.arange(expert_count * capacity, dtype=jnp.int32)
    pick = [(slot_pair[:, k][:, None] == slots[None, :]) for k in range(route_count)]
    pick_any = functools.reduce(jnp.logical_or, pick).astype(jnp.bfloat16)

    def dispatch(rows):
        packed = dot32(pick_any, rows, "ts,td->sd").astype(jnp.bfloat16)
        return lax.all_to_all(
            packed.reshape(expert_count, capacity, model_width),
            "expert",
            split_axis=0,
            concat_axis=0,
            tiled=True,
        ).reshape(expert_count * capacity, model_width)

    def give_back(rows):
        return lax.all_to_all(
            rows.reshape(expert_count, capacity, model_width),
            "expert",
            split_axis=0,
            concat_axis=0,
            tiled=True,
        ).reshape(expert_count * capacity, model_width)

    slot_gates = functools.reduce(
        jnp.add,
        [jnp.sum(jnp.where(pick[k], gate_weights[:, k][:, None], 0.0), axis=0) for k in range(2)],
    )
    slot_gates = lax.all_to_all(
        slot_gates.reshape(expert_count, capacity), "expert", 0, 0, tiled=True
    ).reshape(-1)
    cotangent_rows = dispatch(cotangent)
    rows_in = dispatch(normed_ffn)
    grad_rows_out = (slot_gates[:, None] * cotangent_rows.astype(jnp.float32)).astype(jnp.bfloat16)
    gate_proj = [dot32(rows_in, w, "rd,df->rf") for w in gate_pieces]
    up_proj = [dot32(rows_in, w, "rd,df->rf") for w in up_pieces]
    hidden = [gated_unit(a, b).astype(jnp.bfloat16) for a, b in zip(gate_proj, up_proj)]
    down_sum = sum(dot32(x, w, "rf,fd->rd") for x, w in zip(hidden, down_pieces))
    returned = give_back(down_sum.astype(jnp.bfloat16))
    routed_out = jnp.stack(
        [dot32(p.astype(jnp.bfloat16), returned, "ts,sd->td") for p in pick], axis=1
    )
    mixed_out = hidden_one + jnp.sum(gate_weights[:, :, None] * routed_out, axis=1)
    output = mixed_out.astype(jnp.bfloat16)
    grad_mixed = cotangent.astype(jnp.float32)
    grad_gate_weights = jnp.sum(grad_mixed[:, None, :] * routed_out, axis=2)
    grad_chosen = gate_weights * (
        grad_gate_weights - jnp.sum(gate_weights * grad_gate_weights, axis=1, keepdims=True)
    )
    grad_logits = jnp.sum(jnp.where(chosen_mask, grad_chosen[:, :, None], 0.0), axis=1).astype(
        jnp.bfloat16
    )
    grad_router_full = jnp.einsum(
        "td,te->de", normed_ffn, grad_logits, preferred_element_type=jnp.float32
    )
    grad_normed_ffn = jnp.einsum(
        "te,de->td", grad_logits, full_router, preferred_element_type=jnp.float32
    )
    gate_low, up_low, grad_input = [], [], 0.0
    for r in range(len(hidden)):
        grad_hid = dot32(grad_rows_out, down_pieces[r], "rd,fd->rf")
        unused, pullback = jax.vjp(gated_unit, gate_proj[r], up_proj[r])
        grad_gate_f, grad_up_f = pullback(grad_hid)
        gate_low.append(grad_gate_f.astype(jnp.bfloat16))
        up_low.append(grad_up_f.astype(jnp.bfloat16))
        grad_input = grad_input + dot32(gate_low[r], gate_pieces[r], "rf,df->rd")
        grad_input = grad_input + dot32(up_low[r], up_pieces[r], "rf,df->rd")
    grad_back = give_back(grad_input.astype(jnp.bfloat16))
    grad_gate_w = reduce_pieces([dot32(rows_in, x, "rd,rf->df") for x in gate_low])[None]
    grad_up_w = reduce_pieces([dot32(rows_in, x, "rd,rf->df") for x in up_low])[None]
    grad_down_w = reduce_pieces([dot32(x, grad_rows_out, "rf,rd->fd") for x in hidden])[None]
    grad_normed_ffn = grad_normed_ffn + dot32(pick_any, grad_back, "ts,sd->td")
    grad_two, grad_gain_ffn_full = norm_backward(grad_normed_ffn, normed_two, inverse_two, ffn_gain)
    grad_hidden_one = grad_mixed + grad_two
    grad_attn_low = grad_hidden_one.astype(jnp.bfloat16)
    grad_out_full = jnp.einsum(
        "td,te->de", attended, grad_attn_low, preferred_element_type=jnp.float32
    )
    grad_attended = jnp.einsum(
        "te,de->td", grad_attn_low, full_out, preferred_element_type=jnp.float32
    ).astype(jnp.bfloat16)
    early = (
        reduce_rows(grad_out_full, shard_index).astype(jnp.bfloat16),
        lax.psum_scatter(
            grad_router_full.astype(jnp.bfloat16), "shard", scatter_dimension=0, tiled=True
        ),
        lax.psum_scatter(
            grad_gain_ffn_full.astype(jnp.bfloat16), "shard", scatter_dimension=0, tiled=True
        ),
    )
    early = lax.psum(early, "expert")
    grad_query, grad_keys, grad_values, diag = attend_back(
        info, qkv, kv, grad_attended, attended, logs, vectors
    )
    grad_table_full = table_gradient(diag, bucket_count)
    grad_kv_local = reduce_rows(jnp.concatenate([grad_keys, grad_values], axis=1), shard_index)
    grad_qkv_cols = jnp.concatenate([grad_query, grad_kv_local.astype(jnp.bfloat16)], axis=1)
    grad_qkv_full = jnp.einsum(
        "td,te->de", normed_attn, grad_qkv_cols, preferred_element_type=jnp.float32
    )
    grad_normed_attn = jnp.einsum(
        "te,de->td", grad_qkv_cols, full_qkv, preferred_element_type=jnp.float32
    )
    grad_one, grad_gain_attn_full = norm_backward(
        grad_normed_attn, normed_one, inverse_one, attn_gain
    )
    grad_tokens = grad_hidden_one + grad_one
    late = (
        reduce_rows(grad_qkv_full, shard_index).astype(jnp.bfloat16),
        lax.psum_scatter(
            grad_gain_attn_full.astype(jnp.bfloat16), "shard", scatter_dimension=0, tiled=True
        ),
        lax.psum_scatter(
            grad_table_full.astype(jnp.bfloat16), "shard", scatter_dimension=0, tiled=True
        ),
    )
    late = lax.psum(late, "expert")
    pieces = [x.astype(jnp.float32) for x in (late[0], *early[:2], late[1], early[2], late[2])]
    return (
        output,
        grad_tokens,
        pieces[0],
        pieces[1],
        pieces[2],
        pieces[3],
        pieces[4],
        pieces[5],
        grad_gate_w,
        grad_up_w,
        grad_down_w,
    )


def solution(mesh):
    in_specs = (
        P(("expert", "shard"), None),
        P("shard", None),
        P("shard", None),
        P("shard", None),
        P("shard"),
        P("shard"),
        P("shard", None),
        P("expert", None, "shard"),
        P("expert", None, "shard"),
        P("expert", "shard", None),
        P(("expert", "shard"), None),
        P("expert", None),
        P(("expert", "shard"), None),
    )
    out_specs = (
        P(("expert", "shard"), None),
        P(("expert", "shard"), None),
        P("shard", None),
        P("shard", None),
        P("shard", None),
        P("shard"),
        P("shard"),
        P("shard", None),
        P("expert", None, "shard"),
        P("expert", None, "shard"),
        P("expert", "shard", None),
    )
    return jax.shard_map(local, mesh=mesh, in_specs=in_specs, out_specs=out_specs, check_vma=False)
```

```python
import functools

import jax
import jax.numpy as jnp
from jax import lax
from jax.experimental import pallas as pl
from jax.experimental.pallas import tpu as pltpu
from jax.sharding import PartitionSpec as P

norm_epsilon = 1e-06
bucket_borders = (16, 23, 32, 45, 64, 91, 128, 181, 256, 362, 512, 724, 1024, 1448, 2048, 2896)


def bucket_of(distance):
    clipped = jnp.maximum(distance, 0)
    bucket_id = jnp.minimum(clipped, 15)
    for border in bucket_borders:
        bucket_id = bucket_id + (clipped >= border).astype(jnp.int32)
    return bucket_id


tile = 256
low_score = -1e30


def toeplitz_vectors(bias_table, diagonals):
    offsets = jnp.arange(2 * tile, dtype=jnp.int32)
    offsets = jnp.where(offsets < tile, offsets, offsets - 2 * tile)
    distance = jnp.arange(diagonals, dtype=jnp.int32)[:, None] * tile + offsets[None, :]
    onehot = bucket_of(distance)[None] == jnp.arange(bias_table.shape[1])[:, None, None]
    return jnp.einsum(
        "hc,cdm->hdm", bias_table, onehot.astype(jnp.bfloat16), preferred_element_type=jnp.float32
    )


def fill_bias(vector_ref, head, bias_ref, diagonals):
    def fill(delta, carry):
        row = vector_ref[head, pl.ds(delta, 1), :]
        wide = jnp.broadcast_to(row, (tile, 2 * tile))
        rolled = pltpu.roll(wide, 0, 1, stride=1, stride_axis=0)
        bias_ref[delta] = rolled[:, :tile]
        return carry

    lax.fori_loop(0, diagonals, fill, 0)


def start_of(position, first_end, second_end):
    return jnp.where(
        position >= second_end, second_end, jnp.where(position >= first_end, first_end, 0)
    )


def contract(left, right, left_dim, right_dim):
    return lax.dot_general(
        left, right, (((left_dim,), (right_dim,)), ((), ())), preferred_element_type=jnp.float32
    )


def attend_kernel(info_ref, q_ref, k_ref, v_ref, vector_ref, out_ref, log_ref, bias_ref):
    diagonals = vector_ref.shape[1]
    per_device = q_ref.shape[3] // tile
    first_end, second_end = info_ref[0], info_ref[1]
    fill_bias(vector_ref, 0, bias_ref, diagonals)

    def place(index):
        return index // per_device, pl.ds(pl.multiple_of(index % per_device * tile, tile), tile)

    def query_step(query_tile, carry):
        owner, lanes = place(query_tile)
        query = (q_ref[owner, 0, :, lanes] * 0.125).astype(jnp.bfloat16)
        first_tile = start_of(query_tile * tile, first_end, second_end) // tile
        query_pos = query_tile * tile + lax.broadcasted_iota(jnp.int32, (1, tile), 1)
        query_start = start_of(query_pos, first_end, second_end)

        def step(index, carry):
            top, total, blend = carry
            key_owner, keys = place(index)
            key_pos = index * tile + lax.broadcasted_iota(jnp.int32, (tile, 1), 0)
            scores = contract(k_ref[key_owner, 0, :, keys], query, 0, 0)
            scores = scores + bias_ref[query_tile - index]
            allowed = (key_pos >= query_start) & (key_pos <= query_pos)
            scores = jnp.where(allowed, scores, low_score)
            new_top = jnp.maximum(top, jnp.max(scores, axis=0, keepdims=True))
            weights = jnp.exp(scores - new_top)
            scale = jnp.exp(top - new_top)
            total = total * scale + jnp.sum(weights, axis=0, keepdims=True)
            part = contract(v_ref[key_owner, 0, :, keys], weights.astype(jnp.bfloat16), 1, 0)
            return new_top, total, blend * scale + part

        top, total, blend = lax.fori_loop(
            first_tile,
            query_tile + 1,
            step,
            (
                jnp.full((1, tile), low_score, jnp.float32),
                jnp.zeros((1, tile), jnp.float32),
                jnp.zeros((q_ref.shape[2], tile), jnp.float32),
            ),
        )
        out_ref[owner, 0, :, lanes] = (blend / total).astype(jnp.bfloat16)
        log_ref[0, pl.ds(query_tile, 1), :] = top + jnp.log(total)
        return carry

    lax.fori_loop(0, diagonals, query_step, 0)


def attend_back_kernel(
    info_ref,
    q_ref,
    k_ref,
    v_ref,
    g_ref,
    o_ref,
    log_ref,
    vector_ref,
    dq_ref,
    dk_ref,
    dv_ref,
    diag_ref,
    bias_ref,
    grad_bias_ref,
    dk_acc,
    dv_acc,
):
    diagonals = vector_ref.shape[1]
    per_device = q_ref.shape[3] // tile
    first_end, second_end = info_ref[0], info_ref[1]
    dk_acc[...] = jnp.zeros_like(dk_acc)
    dv_acc[...] = jnp.zeros_like(dv_acc)
    grad_bias_ref[...] = jnp.zeros_like(grad_bias_ref)
    fill_bias(vector_ref, 0, bias_ref, diagonals)

    def place(index):
        return index // per_device, pl.ds(pl.multiple_of(index % per_device * tile, tile), tile)

    def query_step(query_tile, carry):
        owner, lanes = place(query_tile)
        query = (q_ref[owner, 0, :, lanes] * 0.125).astype(jnp.bfloat16)
        grad = g_ref[owner, 0, :, lanes]
        product = grad.astype(jnp.float32) * o_ref[owner, 0, :, lanes].astype(jnp.float32)
        delta_row = jnp.sum(product, axis=0, keepdims=True)
        log_row = log_ref[0, pl.ds(query_tile, 1), :]
        first_tile = start_of(query_tile * tile, first_end, second_end) // tile
        query_pos = query_tile * tile + lax.broadcasted_iota(jnp.int32, (1, tile), 1)
        query_start = start_of(query_pos, first_end, second_end)

        def step(index, dq):
            key_owner, keys = place(index)
            key_pos = index * tile + lax.broadcasted_iota(jnp.int32, (tile, 1), 0)
            key = k_ref[key_owner, 0, :, keys]
            scores = contract(key, query, 0, 0) + bias_ref[query_tile - index]
            allowed = (key_pos >= query_start) & (key_pos <= query_pos)
            probs = jnp.exp(jnp.where(allowed, scores - log_row, low_score))
            grad_probs = contract(v_ref[key_owner, 0, :, keys], grad, 0, 0)
            grad_scores = probs * (grad_probs - delta_row)
            grad_bias_ref[query_tile - index] += grad_scores
            low = grad_scores.astype(jnp.bfloat16)
            dv_acc[index] += contract(grad, probs.astype(jnp.bfloat16), 1, 1)
            dk_acc[index] += contract(query, low, 1, 1)
            return dq + contract(key, low, 1, 0)

        dq = lax.fori_loop(
            first_tile, query_tile + 1, step, jnp.zeros((q_ref.shape[2], tile), jnp.float32)
        )
        dq_ref[owner, 0, :, lanes] = (dq * 0.125).astype(jnp.bfloat16)
        return carry

    lax.fori_loop(0, diagonals, query_step, 0)

    def reduce(delta, carry):
        value = grad_bias_ref[delta]
        value = jnp.concatenate([value, jnp.zeros_like(value)], axis=1)
        half = tile // 2
        while half >= 8:
            value = value[:half] + pltpu.roll(value[half:], 2 * tile - half, 1)
            half //= 2
        diag_ref[0, delta] = value
        return carry

    lax.fori_loop(0, diagonals, reduce, 0)
    for index in range(diagonals):
        owner = index // per_device
        lanes = pl.ds(index % per_device * tile, tile)
        dk_ref[owner, 0, :, lanes] = dk_acc[index].astype(jnp.bfloat16)
        dv_ref[owner, 0, :, lanes] = dv_acc[index].astype(jnp.bfloat16)


def part_spec(shape, part, heads):
    return pl.BlockSpec((shape[0], 1, *shape[2:]), lambda h: (0, h + part * heads, 0, 0))


def attend(info, qkv, vectors):
    devices, parts, head_dim, tok_count = qkv.shape
    heads, diagonals = parts // 3, vectors.shape[1]
    pairs = heads * (devices * tok_count) ** 2 * head_dim
    return pl.pallas_call(
        attend_kernel,
        grid=(heads,),
        in_specs=[
            pl.BlockSpec(memory_space=pltpu.SMEM),
            *(part_spec(qkv.shape, part, heads) for part in range(3)),
            pl.BlockSpec((1, diagonals, 2 * tile), lambda h: (h, 0, 0)),
        ],
        out_specs=[
            part_spec(qkv.shape, 0, heads),
            pl.BlockSpec((1, diagonals, tile), lambda h: (h, 0, 0)),
        ],
        out_shape=[
            jax.ShapeDtypeStruct((devices, heads, head_dim, tok_count), jnp.bfloat16),
            jax.ShapeDtypeStruct((heads, diagonals, tile), jnp.float32),
        ],
        scratch_shapes=[pltpu.VMEM((diagonals, tile, tile), jnp.float32)],
        compiler_params=pltpu.CompilerParams(vmem_limit_bytes=40 * 2**20),
        cost_estimate=pl.CostEstimate(
            flops=16 * 4 * pairs, bytes_accessed=2 * qkv.size, transcendentals=0
        ),
        name="attend",
    )(info, qkv, qkv, qkv, vectors)


def attend_back(info, qkv, grad, attended, logs, vectors):
    devices, parts, head_dim, tok_count = qkv.shape
    heads, diagonals = parts // 3, vectors.shape[1]
    pairs = heads * (devices * tok_count) ** 2 * head_dim
    one = part_spec(qkv.shape, 0, heads)
    return pl.pallas_call(
        attend_back_kernel,
        grid=(heads,),
        in_specs=[
            pl.BlockSpec(memory_space=pltpu.SMEM),
            *(part_spec(qkv.shape, part, heads) for part in range(3)),
            one,
            one,
            pl.BlockSpec((1, diagonals, tile), lambda h: (h, 0, 0)),
            pl.BlockSpec((1, diagonals, 2 * tile), lambda h: (h, 0, 0)),
        ],
        out_specs=[
            one,
            one,
            one,
            pl.BlockSpec((1, diagonals, 8, 2 * tile), lambda h: (h, 0, 0, 0)),
        ],
        out_shape=[jax.ShapeDtypeStruct((devices, heads, head_dim, tok_count), jnp.bfloat16)] * 3
        + [jax.ShapeDtypeStruct((heads, diagonals, 8, 2 * tile), jnp.float32)],
        scratch_shapes=[
            pltpu.VMEM((diagonals, tile, tile), jnp.float32),
            pltpu.VMEM((diagonals, tile, tile), jnp.float32),
            pltpu.VMEM((diagonals, head_dim, tile), jnp.float32),
            pltpu.VMEM((diagonals, head_dim, tile), jnp.float32),
        ],
        compiler_params=pltpu.CompilerParams(vmem_limit_bytes=48 * 2**20),
        cost_estimate=pl.CostEstimate(
            flops=16 * 10 * pairs, bytes_accessed=4 * qkv.size, transcendentals=0
        ),
        name="attend_back",
    )(info, qkv, qkv, qkv, grad, attended, logs, vectors)


def table_gradient(diag, bucket_count):
    head_count, diagonals, fold, width = diag.shape
    offsets = jnp.arange(width, dtype=jnp.int32)
    offsets = jnp.where(offsets < tile, offsets, offsets - width)
    distance = (
        jnp.arange(diagonals, dtype=jnp.int32)[:, None, None] * tile
        + offsets[None, None, :]
        - jnp.arange(fold, dtype=jnp.int32)[None, :, None]
    )
    onehot = bucket_of(distance)[None] == jnp.arange(bucket_count)[:, None, None, None]
    return jnp.einsum(
        "hdrc,bdrc->hb",
        diag,
        onehot.astype(jnp.float32),
        precision=lax.Precision.HIGHEST,
        preferred_element_type=jnp.float32,
    )


def partner(value, flip):
    count = lax.axis_size("shard")
    return lax.ppermute(value, "shard", [(i, i ^ flip) for i in range(count)])


def reduce_near(pieces):
    low = [p.astype(jnp.bfloat16) for p in pieces]
    far = (pieces[2] + partner(low[3], 1).astype(jnp.float32)).astype(jnp.bfloat16)
    near = pieces[0] + partner(low[1], 1).astype(jnp.float32)
    return near, partner(far, 2)


def reduce_pieces(pieces):
    near, far = reduce_near(pieces)
    return near + far.astype(jnp.float32)


def swap_heads(value):
    return lax.all_to_all(value, "shard", split_axis=0, concat_axis=0, tiled=True)


def reduce_rows(value, shard_index):
    count = lax.axis_size("shard")
    split = value.reshape(count, value.shape[0] // count, *value.shape[1:])
    return reduce_pieces(
        [
            lax.dynamic_index_in_dim(split, shard_index ^ r, 0, keepdims=False).astype(jnp.float32)
            for r in range(count)
        ]
    )


def dot32(left, right, spec):
    return jnp.einsum(spec, left, right, preferred_element_type=jnp.float32)


def norm_forward(values):
    inverse = lax.rsqrt(jnp.mean(values * values, axis=-1, keepdims=True) + norm_epsilon)
    return (values * inverse, inverse)


def norm_backward(grad_normed, normalized, inverse, gain_vector):
    grad_gain = jnp.sum(grad_normed * normalized, axis=0)
    scaled = grad_normed * gain_vector
    grad_values = inverse * (
        scaled - normalized * jnp.mean(scaled * normalized, axis=-1, keepdims=True)
    )
    return (grad_values, grad_gain)


def gated_unit(gate_value, up_value):
    return jax.nn.gelu(gate_value) * up_value


def local(
    tokens,
    w_qkv,
    w_out,
    router,
    gain_attn,
    gain_ffn,
    rel_bias,
    w_gate,
    w_up,
    w_down,
    routes,
    lengths,
    cotangent,
):
    shard_index = lax.axis_index("shard")
    full_qkv, full_out, full_router, full_gain_attn, full_gain_ffn = (
        lax.all_gather(w_qkv, "shard", axis=0, tiled=True),
        lax.all_gather(w_out, "shard", axis=0, tiled=True),
        lax.all_gather(router, "shard", axis=0, tiled=True),
        lax.all_gather(gain_attn, "shard", axis=0, tiled=True),
        lax.all_gather(gain_ffn, "shard", axis=0, tiled=True),
    )
    tok_count, model_width = tokens.shape
    local_heads, bucket_count = rel_bias.shape
    shard_count = lax.axis_size("shard")
    head_dim = model_width // (local_heads * shard_count)
    expert_count = full_router.shape[1]
    route_count = routes.shape[1]
    capacity = 2 * route_count * tok_count // expert_count
    inputs = tokens.astype(jnp.float32)
    attn_gain = full_gain_attn.astype(jnp.float32)
    ffn_gain = full_gain_ffn.astype(jnp.float32)
    normed_one, inverse_one = norm_forward(inputs)
    normed_attn = (normed_one * attn_gain).astype(jnp.bfloat16)
    qkv = dot32(full_qkv, normed_attn, "df,td->ft").astype(jnp.bfloat16)
    qkv = qkv.reshape(3, shard_count, local_heads, head_dim, tok_count)
    qkv = qkv.transpose(1, 0, 2, 3, 4)
    qkv = swap_heads(qkv.reshape(shard_count, 3 * local_heads, head_dim, tok_count))
    group_tok = shard_count * tok_count
    info = jnp.stack([lengths[0, 0], lengths[0, 0] + lengths[0, 1]]).astype(jnp.int32)
    vectors = toeplitz_vectors(rel_bias, group_tok // tile)
    weights_in = (w_gate[0], w_up[0], w_down[0])
    across = tuple(partner(w, 2) for w in weights_in)
    attended_group, logs = attend(info, qkv, vectors)
    attended_group, across = lax.optimization_barrier((attended_group, across))
    gate_pieces, up_pieces, down_pieces = (
        [w, partner(w, 1), x, partner(x, 1)] for w, x in zip(weights_in, across)
    )
    attended = swap_heads(attended_group).reshape(model_width, tok_count)
    hidden_one = inputs + dot32(attended, full_out, "dt,de->te")
    normed_two, inverse_two = norm_forward(hidden_one)
    normed_ffn = (normed_two * ffn_gain).astype(jnp.bfloat16)
    logits = jnp.dot(normed_ffn, full_router, preferred_element_type=jnp.float32)
    expert_ids = jnp.arange(expert_count, dtype=jnp.int32)
    chosen_mask = routes[:, :, None] == expert_ids[None, None, :]
    chosen = jnp.sum(jnp.where(chosen_mask, logits[:, None, :], 0.0), axis=2)
    gate_weights = jax.nn.softmax(chosen, axis=1)
    flat_routes = routes.reshape(-1)
    onehot_rows = (flat_routes[:, None] == expert_ids[None, :]).astype(jnp.int32)
    earlier = jnp.cumsum(onehot_rows, axis=0) - onehot_rows
    position = jnp.sum(earlier * onehot_rows, axis=1)
    slot_index = flat_routes * capacity + position
    slot_pair = slot_index.reshape(tok_count, route_count)
    slots = jnp.arange(expert_count * capacity, dtype=jnp.int32)
    pick = [(slot_pair[:, k][:, None] == slots[None, :]) for k in range(route_count)]
    pick_any = functools.reduce(jnp.logical_or, pick).astype(jnp.bfloat16)

    def dispatch(rows):
        packed = dot32(pick_any, rows, "ts,td->sd").astype(jnp.bfloat16)
        return lax.all_to_all(
            packed.reshape(expert_count, capacity, model_width),
            "expert",
            split_axis=0,
            concat_axis=0,
            tiled=True,
        ).reshape(expert_count * capacity, model_width)

    def give_back(rows):
        return lax.all_to_all(
            rows.reshape(expert_count, capacity, model_width),
            "expert",
            split_axis=0,
            concat_axis=0,
            tiled=True,
        ).reshape(expert_count * capacity, model_width)

    slot_gates = functools.reduce(
        jnp.add,
        [jnp.sum(jnp.where(pick[k], gate_weights[:, k][:, None], 0.0), axis=0) for k in range(2)],
    )
    slot_gates = lax.all_to_all(
        slot_gates.reshape(expert_count, capacity), "expert", 0, 0, tiled=True
    ).reshape(-1)
    cotangent_rows = dispatch(cotangent)
    rows_in = dispatch(normed_ffn)
    grad_rows_out = (slot_gates[:, None] * cotangent_rows.astype(jnp.float32)).astype(jnp.bfloat16)
    gate_proj = [dot32(rows_in, w, "rd,df->rf") for w in gate_pieces]
    up_proj = [dot32(rows_in, w, "rd,df->rf") for w in up_pieces]
    hidden = [gated_unit(a, b).astype(jnp.bfloat16) for a, b in zip(gate_proj, up_proj)]
    down_sum = sum(dot32(x, w, "rf,fd->rd") for x, w in zip(hidden, down_pieces))
    returned = give_back(down_sum.astype(jnp.bfloat16))
    routed_out = jnp.stack(
        [dot32(p.astype(jnp.bfloat16), returned, "ts,sd->td") for p in pick], axis=1
    )
    mixed_out = hidden_one + jnp.sum(gate_weights[:, :, None] * routed_out, axis=1)
    output = mixed_out.astype(jnp.bfloat16)
    grad_mixed = cotangent.astype(jnp.float32)
    grad_gate_weights = jnp.sum(grad_mixed[:, None, :] * routed_out, axis=2)
    grad_chosen = gate_weights * (
        grad_gate_weights - jnp.sum(gate_weights * grad_gate_weights, axis=1, keepdims=True)
    )
    grad_logits = jnp.sum(jnp.where(chosen_mask, grad_chosen[:, :, None], 0.0), axis=1).astype(
        jnp.bfloat16
    )
    grad_router_full = jnp.einsum(
        "td,te->de", normed_ffn, grad_logits, preferred_element_type=jnp.float32
    )
    grad_normed_ffn = jnp.einsum(
        "te,de->td", grad_logits, full_router, preferred_element_type=jnp.float32
    )
    gate_low, up_low, grad_input = [], [], 0.0
    for r in range(len(hidden)):
        grad_hid = dot32(grad_rows_out, down_pieces[r], "rd,fd->rf")
        unused, pullback = jax.vjp(gated_unit, gate_proj[r], up_proj[r])
        grad_gate_f, grad_up_f = pullback(grad_hid)
        gate_low.append(grad_gate_f.astype(jnp.bfloat16))
        up_low.append(grad_up_f.astype(jnp.bfloat16))
        grad_input = grad_input + dot32(gate_low[r], gate_pieces[r], "rf,df->rd")
        grad_input = grad_input + dot32(up_low[r], up_pieces[r], "rf,df->rd")
    grad_back = give_back(grad_input.astype(jnp.bfloat16))
    grad_gate_w = reduce_near([dot32(rows_in, x, "rd,rf->df") for x in gate_low])
    grad_up_w = reduce_near([dot32(rows_in, x, "rd,rf->df") for x in up_low])
    grad_down_w = reduce_near([dot32(x, grad_rows_out, "rf,rd->fd") for x in hidden])
    grad_normed_ffn = grad_normed_ffn + dot32(pick_any, grad_back, "ts,sd->td")
    grad_two, grad_gain_ffn_full = norm_backward(grad_normed_ffn, normed_two, inverse_two, ffn_gain)
    grad_hidden_one = grad_mixed + grad_two
    grad_attn_low = grad_hidden_one.astype(jnp.bfloat16)
    grad_out_full = dot32(attended, grad_attn_low, "dt,te->de")
    grad_attended = dot32(full_out, grad_attn_low, "de,te->dt").astype(jnp.bfloat16)
    grad_group = swap_heads(grad_attended.reshape(attended_group.shape))
    filler = jnp.zeros((model_width, -(expert_count + 1) % 128), jnp.float32)
    early = jnp.concatenate(
        [grad_out_full, grad_router_full, grad_gain_ffn_full[:, None], filler], axis=1
    )
    early = lax.psum(reduce_rows(early, shard_index).astype(jnp.bfloat16), "expert")
    grad_query, grad_keys, grad_values, diag = attend_back(
        info, qkv, grad_group, attended_group, logs, vectors
    )
    grad_table = table_gradient(diag, bucket_count)
    grad_cols = jnp.concatenate([grad_query, grad_keys, grad_values], axis=1)
    grad_cols, early, grad_gate_w, grad_up_w, grad_down_w = lax.optimization_barrier(
        (grad_cols, early, grad_gate_w, grad_up_w, grad_down_w)
    )
    early = early.astype(jnp.float32)
    grad_gate_w, grad_up_w, grad_down_w = (
        (near + far.astype(jnp.float32))[None]
        for near, far in (grad_gate_w, grad_up_w, grad_down_w)
    )
    grad_cols = swap_heads(grad_cols).reshape(shard_count, 3, local_heads, head_dim, tok_count)
    grad_cols = grad_cols.transpose(1, 0, 2, 3, 4).reshape(3 * model_width, tok_count)
    grad_qkv_full = dot32(normed_attn, grad_cols, "td,ft->df")
    grad_normed_attn = dot32(grad_cols, full_qkv, "ft,df->td")
    grad_one, grad_gain_attn_full = norm_backward(
        grad_normed_attn, normed_one, inverse_one, attn_gain
    )
    grad_tokens = grad_hidden_one + grad_one
    filler = jnp.zeros((model_width, 127), jnp.float32)
    late = jnp.concatenate([grad_qkv_full, grad_gain_attn_full[:, None], filler], axis=1)
    late = reduce_rows(late, shard_index)
    table_column = jnp.pad(grad_table.reshape(-1), (0, late.shape[0] - grad_table.size))
    late = late + jnp.pad(
        table_column[:, None], ((0, 0), (3 * model_width + 1, late.shape[1] - 3 * model_width - 2))
    )
    late = lax.psum(late.astype(jnp.bfloat16), "expert").astype(jnp.float32)
    pieces = (
        late[:, : 3 * model_width],
        early[:, :model_width],
        early[:, model_width : model_width + expert_count],
        late[:, 3 * model_width],
        early[:, model_width + expert_count],
        late[: grad_table.size, 3 * model_width + 1].reshape(grad_table.shape),
    )
    return (
        output,
        grad_tokens,
        pieces[0],
        pieces[1],
        pieces[2],
        pieces[3],
        pieces[4],
        pieces[5],
        grad_gate_w,
        grad_up_w,
        grad_down_w,
    )


def solution(mesh):
    in_specs = (
        P(("expert", "shard"), None),
        P("shard", None),
        P("shard", None),
        P("shard", None),
        P("shard"),
        P("shard"),
        P("shard", None),
        P("expert", None, "shard"),
        P("expert", None, "shard"),
        P("expert", "shard", None),
        P(("expert", "shard"), None),
        P("expert", None),
        P(("expert", "shard"), None),
    )
    out_specs = (
        P(("expert", "shard"), None),
        P(("expert", "shard"), None),
        P("shard", None),
        P("shard", None),
        P("shard", None),
        P("shard"),
        P("shard"),
        P("shard", None),
        P("expert", None, "shard"),
        P("expert", None, "shard"),
        P("expert", "shard", None),
    )
    return jax.shard_map(local, mesh=mesh, in_specs=in_specs, out_specs=out_specs, check_vma=False)
```

```python
import functools

import jax
import jax.numpy as jnp
from jax import lax
from jax.experimental import pallas as pl
from jax.experimental.pallas import tpu as pltpu
from jax.sharding import PartitionSpec as P

norm_epsilon = 1e-06
bucket_borders = (16, 23, 32, 45, 64, 91, 128, 181, 256, 362, 512, 724, 1024, 1448, 2048, 2896)


def bucket_of(distance):
    clipped = jnp.maximum(distance, 0)
    bucket_id = jnp.minimum(clipped, 15)
    for border in bucket_borders:
        bucket_id = bucket_id + (clipped >= border).astype(jnp.int32)
    return bucket_id


tile = 256
low_score = -1e30


def toeplitz_vectors(bias_table, diagonals):
    offsets = jnp.arange(2 * tile, dtype=jnp.int32)
    offsets = jnp.where(offsets < tile, offsets, offsets - 2 * tile)
    distance = jnp.arange(diagonals, dtype=jnp.int32)[:, None] * tile + offsets[None, :]
    onehot = bucket_of(distance)[None] == jnp.arange(bias_table.shape[1])[:, None, None]
    return jnp.einsum(
        "hc,cdm->hdm", bias_table, onehot.astype(jnp.bfloat16), preferred_element_type=jnp.float32
    )


def fill_bias(vector_ref, head, bias_ref, diagonals):
    def fill(delta, carry):
        row = vector_ref[head, pl.ds(delta, 1), :]
        wide = jnp.broadcast_to(row, (tile, 2 * tile))
        rolled = pltpu.roll(wide, 0, 1, stride=1, stride_axis=0)
        bias_ref[delta] = rolled[:, :tile]
        return carry

    lax.fori_loop(0, diagonals, fill, 0)


def start_of(position, first_end, second_end):
    return jnp.where(
        position >= second_end, second_end, jnp.where(position >= first_end, first_end, 0)
    )


def contract(left, right, left_dim, right_dim):
    return lax.dot_general(
        left, right, (((left_dim,), (right_dim,)), ((), ())), preferred_element_type=jnp.float32
    )


def attend_kernel(info_ref, q_ref, k_ref, v_ref, vector_ref, out_ref, log_ref, bias_ref):
    diagonals = vector_ref.shape[1]
    per_device = q_ref.shape[3] // tile
    first_end, second_end = info_ref[0], info_ref[1]
    fill_bias(vector_ref, 0, bias_ref, diagonals)

    def place(index):
        return index // per_device, pl.ds(pl.multiple_of(index % per_device * tile, tile), tile)

    def query_step(query_tile, carry):
        owner, lanes = place(query_tile)
        query = (q_ref[owner, 0, :, lanes] * 0.125).astype(jnp.bfloat16)
        first_tile = start_of(query_tile * tile, first_end, second_end) // tile
        query_pos = query_tile * tile + lax.broadcasted_iota(jnp.int32, (1, tile), 1)
        query_start = start_of(query_pos, first_end, second_end)

        def step(index, carry):
            top, total, blend = carry
            key_owner, keys = place(index)
            key_pos = index * tile + lax.broadcasted_iota(jnp.int32, (tile, 1), 0)
            scores = contract(k_ref[key_owner, 0, :, keys], query, 0, 0)
            scores = scores + bias_ref[query_tile - index]
            allowed = (key_pos >= query_start) & (key_pos <= query_pos)
            scores = jnp.where(allowed, scores, low_score)
            new_top = jnp.maximum(top, jnp.max(scores, axis=0, keepdims=True))
            weights = jnp.exp(scores - new_top)
            scale = jnp.exp(top - new_top)
            total = total * scale + jnp.sum(weights, axis=0, keepdims=True)
            part = contract(v_ref[key_owner, 0, :, keys], weights.astype(jnp.bfloat16), 1, 0)
            return new_top, total, blend * scale + part

        top, total, blend = lax.fori_loop(
            first_tile,
            query_tile + 1,
            step,
            (
                jnp.full((1, tile), low_score, jnp.float32),
                jnp.zeros((1, tile), jnp.float32),
                jnp.zeros((q_ref.shape[2], tile), jnp.float32),
            ),
        )
        out_ref[owner, 0, :, lanes] = (blend / total).astype(jnp.bfloat16)
        log_ref[0, pl.ds(query_tile, 1), :] = top + jnp.log(total)
        return carry

    lax.fori_loop(0, diagonals, query_step, 0)


def attend_back_kernel(
    info_ref,
    q_ref,
    k_ref,
    v_ref,
    g_ref,
    o_ref,
    log_ref,
    vector_ref,
    dq_ref,
    dk_ref,
    dv_ref,
    diag_ref,
    bias_ref,
    grad_bias_ref,
    dk_acc,
    dv_acc,
):
    diagonals = vector_ref.shape[1]
    per_device = q_ref.shape[3] // tile
    first_end, second_end = info_ref[0], info_ref[1]
    dk_acc[...] = jnp.zeros_like(dk_acc)
    dv_acc[...] = jnp.zeros_like(dv_acc)
    grad_bias_ref[...] = jnp.zeros_like(grad_bias_ref)
    fill_bias(vector_ref, 0, bias_ref, diagonals)

    def place(index):
        return index // per_device, pl.ds(pl.multiple_of(index % per_device * tile, tile), tile)

    def query_step(query_tile, carry):
        owner, lanes = place(query_tile)
        query = (q_ref[owner, 0, :, lanes] * 0.125).astype(jnp.bfloat16)
        grad = g_ref[owner, 0, :, lanes]
        product = grad.astype(jnp.float32) * o_ref[owner, 0, :, lanes].astype(jnp.float32)
        delta_row = jnp.sum(product, axis=0, keepdims=True)
        log_row = log_ref[0, pl.ds(query_tile, 1), :]
        first_tile = start_of(query_tile * tile, first_end, second_end) // tile
        query_pos = query_tile * tile + lax.broadcasted_iota(jnp.int32, (1, tile), 1)
        query_start = start_of(query_pos, first_end, second_end)

        def step(index, dq):
            key_owner, keys = place(index)
            key_pos = index * tile + lax.broadcasted_iota(jnp.int32, (tile, 1), 0)
            key = k_ref[key_owner, 0, :, keys]
            scores = contract(key, query, 0, 0) + bias_ref[query_tile - index]
            allowed = (key_pos >= query_start) & (key_pos <= query_pos)
            probs = jnp.exp(jnp.where(allowed, scores - log_row, low_score))
            grad_probs = contract(v_ref[key_owner, 0, :, keys], grad, 0, 0)
            grad_scores = probs * (grad_probs - delta_row)
            grad_bias_ref[query_tile - index] += grad_scores
            low = grad_scores.astype(jnp.bfloat16)
            dv_acc[index] += contract(grad, probs.astype(jnp.bfloat16), 1, 1)
            dk_acc[index] += contract(query, low, 1, 1)
            return dq + contract(key, low, 1, 0)

        dq = lax.fori_loop(
            first_tile, query_tile + 1, step, jnp.zeros((q_ref.shape[2], tile), jnp.float32)
        )
        dq_ref[owner, 0, :, lanes] = (dq * 0.125).astype(jnp.bfloat16)
        return carry

    lax.fori_loop(0, diagonals, query_step, 0)

    def reduce(delta, carry):
        value = grad_bias_ref[delta]
        value = jnp.concatenate([value, jnp.zeros_like(value)], axis=1)
        half = tile // 2
        while half >= 8:
            value = value[:half] + pltpu.roll(value[half:], 2 * tile - half, 1)
            half //= 2
        diag_ref[0, delta] = value
        return carry

    lax.fori_loop(0, diagonals, reduce, 0)
    for index in range(diagonals):
        owner = index // per_device
        lanes = pl.ds(index % per_device * tile, tile)
        dk_ref[owner, 0, :, lanes] = dk_acc[index].astype(jnp.bfloat16)
        dv_ref[owner, 0, :, lanes] = dv_acc[index].astype(jnp.bfloat16)


def part_spec(shape, part, heads):
    return pl.BlockSpec((shape[0], 1, *shape[2:]), lambda h: (0, h + part * heads, 0, 0))


def attend(info, qkv, vectors):
    devices, parts, head_dim, tok_count = qkv.shape
    heads, diagonals = parts // 3, vectors.shape[1]
    pairs = heads * (devices * tok_count) ** 2 * head_dim
    return pl.pallas_call(
        attend_kernel,
        grid=(heads,),
        in_specs=[
            pl.BlockSpec(memory_space=pltpu.SMEM),
            *(part_spec(qkv.shape, part, heads) for part in range(3)),
            pl.BlockSpec((1, diagonals, 2 * tile), lambda h: (h, 0, 0)),
        ],
        out_specs=[
            part_spec(qkv.shape, 0, heads),
            pl.BlockSpec((1, diagonals, tile), lambda h: (h, 0, 0)),
        ],
        out_shape=[
            jax.ShapeDtypeStruct((devices, heads, head_dim, tok_count), jnp.bfloat16),
            jax.ShapeDtypeStruct((heads, diagonals, tile), jnp.float32),
        ],
        scratch_shapes=[pltpu.VMEM((diagonals, tile, tile), jnp.float32)],
        compiler_params=pltpu.CompilerParams(vmem_limit_bytes=40 * 2**20),
        cost_estimate=pl.CostEstimate(
            flops=16 * 4 * pairs, bytes_accessed=2 * qkv.size, transcendentals=0
        ),
        name="attend",
    )(info, qkv, qkv, qkv, vectors)


def attend_back(info, qkv, grad, attended, logs, vectors):
    devices, parts, head_dim, tok_count = qkv.shape
    heads, diagonals = parts // 3, vectors.shape[1]
    pairs = heads * (devices * tok_count) ** 2 * head_dim
    one = part_spec(qkv.shape, 0, heads)
    return pl.pallas_call(
        attend_back_kernel,
        grid=(heads,),
        in_specs=[
            pl.BlockSpec(memory_space=pltpu.SMEM),
            *(part_spec(qkv.shape, part, heads) for part in range(3)),
            one,
            one,
            pl.BlockSpec((1, diagonals, tile), lambda h: (h, 0, 0)),
            pl.BlockSpec((1, diagonals, 2 * tile), lambda h: (h, 0, 0)),
        ],
        out_specs=[
            one,
            one,
            one,
            pl.BlockSpec((1, diagonals, 8, 2 * tile), lambda h: (h, 0, 0, 0)),
        ],
        out_shape=[jax.ShapeDtypeStruct((devices, heads, head_dim, tok_count), jnp.bfloat16)] * 3
        + [jax.ShapeDtypeStruct((heads, diagonals, 8, 2 * tile), jnp.float32)],
        scratch_shapes=[
            pltpu.VMEM((diagonals, tile, tile), jnp.float32),
            pltpu.VMEM((diagonals, tile, tile), jnp.float32),
            pltpu.VMEM((diagonals, head_dim, tile), jnp.float32),
            pltpu.VMEM((diagonals, head_dim, tile), jnp.float32),
        ],
        compiler_params=pltpu.CompilerParams(vmem_limit_bytes=48 * 2**20),
        cost_estimate=pl.CostEstimate(
            flops=16 * 10 * pairs, bytes_accessed=4 * qkv.size, transcendentals=0
        ),
        name="attend_back",
    )(info, qkv, qkv, qkv, grad, attended, logs, vectors)


def table_gradient(diag, bucket_count):
    head_count, diagonals, fold, width = diag.shape
    offsets = jnp.arange(width, dtype=jnp.int32)
    offsets = jnp.where(offsets < tile, offsets, offsets - width)
    distance = (
        jnp.arange(diagonals, dtype=jnp.int32)[:, None, None] * tile
        + offsets[None, None, :]
        - jnp.arange(fold, dtype=jnp.int32)[None, :, None]
    )
    onehot = bucket_of(distance)[None] == jnp.arange(bucket_count)[:, None, None, None]
    return jnp.einsum(
        "hdrc,bdrc->hb",
        diag,
        onehot.astype(jnp.float32),
        precision=lax.Precision.HIGHEST,
        preferred_element_type=jnp.float32,
    )


def partner(value, flip):
    count = lax.axis_size("shard")
    return lax.ppermute(value, "shard", [(i, i ^ flip) for i in range(count)])


def reduce_near(pieces):
    low = [p.astype(jnp.bfloat16) for p in pieces]
    far = (pieces[2] + partner(low[3], 1).astype(jnp.float32)).astype(jnp.bfloat16)
    near = pieces[0] + partner(low[1], 1).astype(jnp.float32)
    return near, far


def reduce_pieces(pieces):
    near, far = reduce_near(pieces)
    return near + partner(far, 2).astype(jnp.float32)


def swap_heads(value):
    return lax.all_to_all(value, "shard", split_axis=0, concat_axis=0, tiled=True)


def reduce_rows(value, columns, shard_index):
    count = lax.axis_size("shard")
    rows = value.shape[0] // count
    filler = jnp.zeros((rows, -columns.shape[1] % 128), jnp.bfloat16)

    def piece(r):
        first = (shard_index ^ r) * rows
        return jnp.concatenate(
            [
                lax.dynamic_slice_in_dim(value, first, rows, 0),
                lax.dynamic_slice_in_dim(columns, first, rows, 0),
                filler,
            ],
            axis=1,
        ).astype(jnp.float32)

    return reduce_pieces([piece(r) for r in range(count)])


def sum_over_expert(value):
    count = lax.axis_size("expert")
    parts = lax.all_to_all(
        value.reshape(count, value.shape[0] // count, value.shape[1]),
        "expert",
        split_axis=0,
        concat_axis=0,
        tiled=True,
    )
    total = jnp.sum(parts.astype(jnp.float32), axis=0).astype(jnp.bfloat16)
    return lax.all_gather(total, "expert", axis=0, tiled=True)


def dot32(left, right, spec):
    return jnp.einsum(spec, left, right, preferred_element_type=jnp.float32)


def norm_forward(values):
    inverse = lax.rsqrt(jnp.mean(values * values, axis=-1, keepdims=True) + norm_epsilon)
    return (values * inverse, inverse)


def norm_backward(grad_normed, normalized, inverse, gain_vector):
    grad_gain = jnp.sum(grad_normed * normalized, axis=0)
    scaled = grad_normed * gain_vector
    grad_values = inverse * (
        scaled - normalized * jnp.mean(scaled * normalized, axis=-1, keepdims=True)
    )
    return (grad_values, grad_gain)


def gated_unit(gate_value, up_value):
    return jax.nn.gelu(gate_value) * up_value


def local(
    tokens,
    w_qkv,
    w_out,
    router,
    gain_attn,
    gain_ffn,
    rel_bias,
    w_gate,
    w_up,
    w_down,
    routes,
    lengths,
    cotangent,
):
    shard_index = lax.axis_index("shard")
    full_qkv, full_out, full_router, full_gain_attn, full_gain_ffn = (
        lax.all_gather(w_qkv, "shard", axis=0, tiled=True),
        lax.all_gather(w_out, "shard", axis=0, tiled=True),
        lax.all_gather(router, "shard", axis=0, tiled=True),
        lax.all_gather(gain_attn, "shard", axis=0, tiled=True),
        lax.all_gather(gain_ffn, "shard", axis=0, tiled=True),
    )
    tok_count, model_width = tokens.shape
    local_heads, bucket_count = rel_bias.shape
    shard_count = lax.axis_size("shard")
    head_dim = model_width // (local_heads * shard_count)
    expert_count = full_router.shape[1]
    route_count = routes.shape[1]
    capacity = 2 * route_count * tok_count // expert_count
    inputs = tokens.astype(jnp.float32)
    attn_gain = full_gain_attn.astype(jnp.float32)
    ffn_gain = full_gain_ffn.astype(jnp.float32)
    normed_one, inverse_one = norm_forward(inputs)
    normed_attn = (normed_one * attn_gain).astype(jnp.bfloat16)
    qkv = dot32(full_qkv, normed_attn, "df,td->ft").astype(jnp.bfloat16)
    qkv = qkv.reshape(3, shard_count, local_heads, head_dim, tok_count)
    qkv = qkv.transpose(1, 0, 2, 3, 4)
    qkv = swap_heads(qkv.reshape(shard_count, 3 * local_heads, head_dim, tok_count))
    group_tok = shard_count * tok_count
    info = jnp.stack([lengths[0, 0], lengths[0, 0] + lengths[0, 1]]).astype(jnp.int32)
    vectors = toeplitz_vectors(rel_bias, group_tok // tile)
    expert_ids = jnp.arange(expert_count, dtype=jnp.int32)
    flat_routes = routes.reshape(-1)
    onehot_rows = (flat_routes[:, None] == expert_ids[None, :]).astype(jnp.int32)
    earlier = jnp.cumsum(onehot_rows, axis=0) - onehot_rows
    position = jnp.sum(earlier * onehot_rows, axis=1)
    slot_index = flat_routes * capacity + position
    slot_pair = slot_index.reshape(tok_count, route_count)
    slots = jnp.arange(expert_count * capacity, dtype=jnp.int32)
    pick = [(slot_pair[:, k][:, None] == slots[None, :]) for k in range(route_count)]
    pick_any = functools.reduce(jnp.logical_or, pick).astype(jnp.bfloat16)

    def dispatch(rows):
        packed = dot32(pick_any, rows, "ts,td->sd").astype(jnp.bfloat16)
        return lax.all_to_all(
            packed.reshape(expert_count, capacity, model_width),
            "expert",
            split_axis=0,
            concat_axis=0,
            tiled=True,
        ).reshape(expert_count * capacity, model_width)

    cotangent_rows = dispatch(cotangent)
    weights_in = (w_gate[0], w_up[0], w_down[0])
    across = tuple(partner(w, 2) for w in weights_in)
    attended_group, logs = attend(info, qkv, vectors)
    attended_group, across_gate, across_up, cotangent_rows, full_out, full_router = (
        lax.optimization_barrier(
            (attended_group, across[0], across[1], cotangent_rows, full_out, full_router)
        )
    )
    attended = swap_heads(attended_group).reshape(model_width, tok_count)
    hidden_one = inputs + dot32(attended, full_out, "dt,de->te")
    hidden_one, across_down = lax.optimization_barrier((hidden_one, across[2]))
    gate_pieces, up_pieces, down_pieces = (
        [w, partner(w, 1), x, partner(x, 1)]
        for w, x in zip(weights_in, (across_gate, across_up, across_down))
    )
    normed_two, inverse_two = norm_forward(hidden_one)
    normed_ffn = (normed_two * ffn_gain).astype(jnp.bfloat16)
    logits = jnp.dot(normed_ffn, full_router, preferred_element_type=jnp.float32)
    chosen_mask = routes[:, :, None] == expert_ids[None, None, :]
    chosen = jnp.sum(jnp.where(chosen_mask, logits[:, None, :], 0.0), axis=2)
    gate_weights = jax.nn.softmax(chosen, axis=1)
    def give_back(rows):
        return lax.all_to_all(
            rows.reshape(expert_count, capacity, model_width),
            "expert",
            split_axis=0,
            concat_axis=0,
            tiled=True,
        ).reshape(expert_count * capacity, model_width)

    slot_gates = functools.reduce(
        jnp.add,
        [jnp.sum(jnp.where(pick[k], gate_weights[:, k][:, None], 0.0), axis=0) for k in range(2)],
    )
    slot_gates = lax.all_to_all(
        slot_gates.reshape(expert_count, capacity), "expert", 0, 0, tiled=True
    ).reshape(-1)
    rows_in = dispatch(normed_ffn)
    grad_rows_out = (slot_gates[:, None] * cotangent_rows.astype(jnp.float32)).astype(jnp.bfloat16)
    gate_proj = [dot32(rows_in, w, "rd,df->rf") for w in gate_pieces]
    up_proj = [dot32(rows_in, w, "rd,df->rf") for w in up_pieces]
    hidden = [gated_unit(a, b).astype(jnp.bfloat16) for a, b in zip(gate_proj, up_proj)]
    down_sum = sum(dot32(x, w, "rf,fd->rd") for x, w in zip(hidden, down_pieces))
    down_low, grad_rows_out = lax.optimization_barrier(
        (down_sum.astype(jnp.bfloat16), grad_rows_out)
    )
    returned = give_back(down_low)
    routed_out = jnp.stack(
        [dot32(p.astype(jnp.bfloat16), returned, "ts,sd->td") for p in pick], axis=1
    )
    mixed_out = hidden_one + jnp.sum(gate_weights[:, :, None] * routed_out, axis=1)
    output = mixed_out.astype(jnp.bfloat16)
    grad_mixed = cotangent.astype(jnp.float32)
    grad_gate_weights = jnp.sum(grad_mixed[:, None, :] * routed_out, axis=2)
    grad_chosen = gate_weights * (
        grad_gate_weights - jnp.sum(gate_weights * grad_gate_weights, axis=1, keepdims=True)
    )
    grad_logits = jnp.sum(jnp.where(chosen_mask, grad_chosen[:, :, None], 0.0), axis=1).astype(
        jnp.bfloat16
    )
    grad_router_full = jnp.einsum(
        "td,te->de", normed_ffn, grad_logits, preferred_element_type=jnp.float32
    )
    grad_normed_ffn = jnp.einsum(
        "te,de->td", grad_logits, full_router, preferred_element_type=jnp.float32
    )
    gate_low, up_low, grad_input = [], [], 0.0
    for r in range(len(hidden)):
        grad_hid = dot32(grad_rows_out, down_pieces[r], "rd,fd->rf")
        unused, pullback = jax.vjp(gated_unit, gate_proj[r], up_proj[r])
        grad_gate_f, grad_up_f = pullback(grad_hid)
        gate_low.append(grad_gate_f.astype(jnp.bfloat16))
        up_low.append(grad_up_f.astype(jnp.bfloat16))
        grad_input = grad_input + dot32(gate_low[r], gate_pieces[r], "rf,df->rd")
        grad_input = grad_input + dot32(up_low[r], up_pieces[r], "rf,df->rd")
    grad_low, rows_in, grad_rows_out = lax.optimization_barrier(
        (grad_input.astype(jnp.bfloat16), rows_in, grad_rows_out)
    )
    grad_back = give_back(grad_low)
    grad_gate_w = reduce_near([dot32(rows_in, x, "rd,rf->df") for x in gate_low])
    grad_up_w = reduce_near([dot32(rows_in, x, "rd,rf->df") for x in up_low])
    grad_down_w = reduce_near([dot32(x, grad_rows_out, "rf,rd->fd") for x in hidden])
    grad_normed_ffn = grad_normed_ffn + dot32(pick_any, grad_back, "ts,sd->td")
    grad_two, grad_gain_ffn_full = norm_backward(grad_normed_ffn, normed_two, inverse_two, ffn_gain)
    grad_hidden_one = grad_mixed + grad_two
    grad_attn_low = grad_hidden_one.astype(jnp.bfloat16)
    grad_out_full = dot32(attended, grad_attn_low, "dt,te->de")
    grad_attended = dot32(full_out, grad_attn_low, "de,te->dt").astype(jnp.bfloat16)
    grad_attended, grad_gate_w, grad_up_w, grad_down_w = lax.optimization_barrier(
        (grad_attended, grad_gate_w, grad_up_w, grad_down_w)
    )
    grad_group = swap_heads(grad_attended.reshape(attended_group.shape))
    grad_gate_w, grad_up_w, grad_down_w = (
        (near, partner(far, 2)) for near, far in (grad_gate_w, grad_up_w, grad_down_w)
    )
    early = reduce_rows(
        grad_out_full.astype(jnp.bfloat16),
        jnp.concatenate([grad_router_full, grad_gain_ffn_full[:, None]], axis=1).astype(
            jnp.bfloat16
        ),
        shard_index,
    )
    early = lax.psum(early.astype(jnp.bfloat16), "expert")
    grad_query, grad_keys, grad_values, diag = attend_back(
        info, qkv, grad_group, attended_group, logs, vectors
    )
    grad_table = table_gradient(diag, bucket_count)
    grad_cols = jnp.concatenate([grad_query, grad_keys, grad_values], axis=1)
    grad_cols, grad_gate_w, grad_up_w, grad_down_w = lax.optimization_barrier(
        (grad_cols, grad_gate_w, grad_up_w, grad_down_w)
    )
    grad_gate_w, grad_up_w, grad_down_w = (
        (near + far.astype(jnp.float32))[None]
        for near, far in (grad_gate_w, grad_up_w, grad_down_w)
    )
    grad_cols, early = lax.optimization_barrier((swap_heads(grad_cols), early))
    early = early.astype(jnp.float32)
    grad_cols = grad_cols.reshape(shard_count, 3, local_heads, head_dim, tok_count)
    grad_cols = grad_cols.transpose(1, 0, 2, 3, 4).reshape(3 * model_width, tok_count)
    grad_qkv_full = dot32(normed_attn, grad_cols, "td,ft->df")
    grad_normed_attn = dot32(grad_cols, full_qkv, "ft,df->td")
    grad_one, grad_gain_attn_full = norm_backward(
        grad_normed_attn, normed_one, inverse_one, attn_gain
    )
    grad_tokens = grad_hidden_one + grad_one
    late = reduce_rows(
        grad_qkv_full.astype(jnp.bfloat16),
        grad_gain_attn_full[:, None].astype(jnp.bfloat16),
        shard_index,
    )
    table_column = jnp.pad(grad_table.reshape(-1), (0, late.shape[0] - grad_table.size))
    late = late + jnp.pad(
        table_column[:, None], ((0, 0), (3 * model_width + 1, late.shape[1] - 3 * model_width - 2))
    )
    row_count = late.shape[0]
    late = late.astype(jnp.bfloat16)
    late = jnp.pad(late, ((0, -row_count % lax.axis_size("expert")), (0, 0)))
    late = sum_over_expert(late)[:row_count].astype(jnp.float32)
    pieces = (
        late[:, : 3 * model_width],
        early[:, :model_width],
        early[:, model_width : model_width + expert_count],
        late[:, 3 * model_width],
        early[:, model_width + expert_count],
        late[: grad_table.size, 3 * model_width + 1].reshape(grad_table.shape),
    )
    return (
        output,
        grad_tokens,
        pieces[0],
        pieces[1],
        pieces[2],
        pieces[3],
        pieces[4],
        pieces[5],
        grad_gate_w,
        grad_up_w,
        grad_down_w,
    )


def solution(mesh):
    in_specs = (
        P(("expert", "shard"), None),
        P("shard", None),
        P("shard", None),
        P("shard", None),
        P("shard"),
        P("shard"),
        P("shard", None),
        P("expert", None, "shard"),
        P("expert", None, "shard"),
        P("expert", "shard", None),
        P(("expert", "shard"), None),
        P("expert", None),
        P(("expert", "shard"), None),
    )
    out_specs = (
        P(("expert", "shard"), None),
        P(("expert", "shard"), None),
        P("shard", None),
        P("shard", None),
        P("shard", None),
        P("shard"),
        P("shard"),
        P("shard", None),
        P("expert", None, "shard"),
        P("expert", None, "shard"),
        P("expert", "shard", None),
    )
    return jax.shard_map(local, mesh=mesh, in_specs=in_specs, out_specs=out_specs, check_vma=False)
```
